32 devices in a mesh: grp: 4 (over y, x), mem: 8 (over z, core).
Axes of the slice: x: 2, y: 2, z: 4, core: 2. Of those that a mesh axis runs over, the one named last changes fastest.
Arguments:
- t_amps: bfloat16 [320, 32, 600], P(('grp', 'mem')), may hold values from -6 to 6
- vvvv: bfloat16 [19200, 9600], P('mem', 'grp'), may hold values from -0.125 to 0.125
- irreps: int32 [600], replicated, may hold values from 0 to 7
Outputs:
- ladder: float32 [320, 9600], P('mem', 'grp')
The draws below stay inside these ranges and needn't reach their ends.
All inputs are finite; a program needn't handle non-finite values.
Results may differ from the reference program's by a relative error of at most 0.0003.
Values may be sent and summed in bfloat16 or wider, within the bound.
No kernel may reach another device: no remote copies, remote signals or barrier semaphores. Data moves between devices by JAX's collectives and lax.ppermute only.
A program may use at most 128 MiB of HBM per device.

```python
import jax
import jax.numpy as jnp
from jax import lax

NV = 600
OP = 320
CW = 32
AW = 16


def set_ends(array, rng, smallest, top_value):
    index_at = [jax.random.randint(jax.random.fold_in(rng, axis), (), 0, length) for axis, length in enumerate(array.shape)]
    widest = array.shape.index(max(array.shape))
    neighbour = index_at[:widest] + [(index_at[widest] + 1) % array.shape[widest]] + index_at[widest + 1:]
    return array.at[tuple(index_at)].set(smallest).at[tuple(neighbour)].set(top_value)


def block_levels(key, dims, split, low, largest):
    def one(dim, parts):
        steps = jax.random.uniform(jax.random.fold_in(jax.random.fold_in(key, 6), dim), (parts,), jnp.float32, low / len(split), largest / len(split))
        return jnp.repeat(jnp.exp(steps), dims[dim] // parts).reshape((-1,) + (1,) * (len(dims) - dim - 1))

    gain = one(*split[0])
    for cut in split[1:]:
        gain = gain * one(*cut)
    return gain


def noise(rng, dims, spread, bound, pieces=(), kind=jnp.bfloat16):
    result = spread * jax.random.normal(rng, dims, jnp.float32)
    if pieces:
        result = result * block_levels(rng, dims, pieces, -0.22, 0.18)
    return jnp.clip(result, -bound, bound).astype(kind)


def setup_inputs(seed: int = 0) -> dict:
    key_list = jax.random.split(jax.random.key(seed), 4)
    return {
        "t_amps": noise(key_list[0], (OP, CW, NV), 1.0, 6.0, ((0, 32),)),
        "vvvv": noise(key_list[1], (CW * NV, AW * NV), (CW * NV // 8) ** -0.5, 0.125, ((0, 8), (1, 4))),
        "irreps": set_ends(jax.random.randint(key_list[2], (NV,), 0, 8), jax.random.fold_in(key_list[2], 1), 0, 7).astype(jnp.int32),
    }


def reference(t_amps, vvvv, irreps):
    pair_a = jnp.bitwise_xor(irreps[:AW][:, None], irreps[None, :]).reshape(-1)

    def contract(index, total):
        rows = lax.dynamic_slice_in_dim(vvvv, index * NV, NV, 0)
        label = lax.dynamic_slice_in_dim(irreps, index, 1, 0)
        pair_c = jnp.bitwise_xor(label, irreps)
        block = jnp.where(pair_c[:, None] == pair_a[None, :], rows, jnp.zeros((), rows.dtype))
        amps = lax.dynamic_index_in_dim(t_amps, index, 1, keepdims=False)
        return total + jnp.dot(amps, block, preferred_element_type=jnp.float32)

    start = jnp.zeros((OP, AW * NV), jnp.float32)
    return lax.fori_loop(0, CW, contract, start)
```

```python
import jax
import jax.numpy as jnp
from jax import lax
from jax.experimental import pallas as pl
from jax.experimental.pallas import tpu as pltpu
from jax.sharding import PartitionSpec as P

LANES = 128
TILE_N = 512
QMAX = 32000.0
STEPS = 8.0


def round_up(value, unit):
    return -(-value // unit) * unit


def partial_kernel(shape, where_ref, *refs):
    grp_count, chips, cc, nv, width = shape
    lhs_refs = refs[:grp_count]
    v_ref, w_ref, row_ref, col_ref, code_ref, own_ref, wide, lhs, masked, scales = refs[grp_count:]
    step = pl.program_id(0)
    group, chip, core = where_ref[0], where_ref[1], where_ref[2]
    rows_each = lhs_refs[0].shape[0]
    half = cc // 2
    depth = masked.shape[1]
    block = code_ref.shape[1]

    @pl.when(step == 0)
    def _():
        for j in range(grp_count):
            wide[j * rows_each:(j + 1) * rows_each, :] = lhs_refs[j][...].astype(jnp.float32)
        lhs[...] = wide[...].astype(jnp.bfloat16)
        masked[...] = jnp.zeros_like(masked)
        scales[...] = jnp.zeros_like(scales)

    for side, source in ((core, v_ref), (1 - core, w_ref)):
        for c in range(half):
            at = side * half + c
            labels = row_ref[at]
            for n in range(0, TILE_N, LANES):
                keep = labels == col_ref[0:1, n:n + LANES]
                masked[at, 0:nv, n:n + LANES] = jnp.where(keep, source[c, :, n:n + LANES], jnp.zeros((), jnp.bfloat16))
    total = jnp.dot(lhs[...], masked[...].reshape(cc * depth, TILE_N), preferred_element_type=jnp.float32)

    lane = lax.broadcasted_iota(jnp.int32, (total.shape[0], LANES), 1)
    exponents = scales[...]
    first = step * (TILE_N // LANES)
    coded = []
    for n in range(0, TILE_N, LANES):
        part = total[:, n:n + LANES]
        top = jnp.maximum(jnp.max(jnp.abs(part), axis=1, keepdims=True), 1e-30)
        level = jnp.ceil(jnp.log2(top) * STEPS + 0.05)
        code = jnp.round(part * (jnp.exp2(level * (-1.0 / STEPS)) * QMAX))
        at = first + n // LANES
        exponents = jnp.where(lane == width % LANES + at, level, exponents)
        is_last = at == width // LANES
        code = jnp.where(jnp.logical_and(is_last, lane >= width % LANES), exponents, code)
        coded.append(code)
    scales[...] = exponents
    per_group = rows_each // block
    for j in range(grp_count):
        for q in range(per_group):
            low = j * rows_each + q * block
            target = jnp.bitwise_xor(jnp.bitwise_xor(group, j) * per_group + q, chip)
            for i, n in enumerate(range(0, TILE_N, LANES)):
                code_ref[target, :, n:n + LANES] = coded[i][low:low + block].astype(jnp.int16)

            @pl.when(target == 0)
            def _():
                own_ref[...] = total[low:low + block]


def combine_kernel(width, own_ref, *refs):
    code_refs, out_ref = refs[:-1], refs[-1]
    base = width // LANES * LANES
    exponents = [jnp.exp2(ref[:, base:base + LANES].astype(jnp.float32) * (1.0 / STEPS)) * (1.0 / QMAX) for ref in code_refs]
    for low in range(0, width, LANES):
        high = min(low + LANES, width)
        at = width % LANES + low // LANES
        value = own_ref[:, low:high]
        for scale, ref in zip(exponents, code_refs):
            value = value + ref[:, low:high].astype(jnp.float32) * scale[:, at:at + 1]
        out_ref[:, low:high] = value


def shards(t_amps, vvvv, irreps):
    mem_count = lax.axis_size("mem")
    grp_count = lax.axis_size("grp")
    per_device, cw, nv = t_amps.shape
    chips = mem_count // 2
    cc = cw // chips
    half = cc // 2
    width = vvvv.shape[1]
    a_local = width // nv
    mem = lax.axis_index("mem")
    group = lax.axis_index("grp")
    chip, core = mem // 2, mem % 2

    def swap(x, axis, k, count):
        return lax.ppermute(x, axis, [(i, i ^ k) for i in range(count)])

    other = swap(vvvv, "mem", 1, mem_count)

    depth = round_up(nv, LANES)
    padded = jnp.pad(t_amps, ((0, 0), (0, 0), (0, depth - nv))).reshape(per_device, chips, cc, depth)

    def slot(m):
        return m // (2 * grp_count) * grp_count + m % grp_count

    pieces = []
    for r in range(chips):
        send = lax.dynamic_index_in_dim(padded, jnp.bitwise_xor(slot(mem), r), 1, keepdims=False)
        perm = [(m, (slot(m) ^ r) * 2 + m // grp_count % 2) for m in range(mem_count)]
        pieces.append(lax.ppermute(send, "mem", perm))
    bit = 1
    while bit < chips:
        flip = jnp.bitwise_and(chip, bit) != 0
        pieces = [jnp.where(flip, pieces[j ^ bit], pieces[j]) for j in range(chips)]
        bit *= 2
    mine = jnp.concatenate(pieces).reshape(chips * per_device, cc * depth)

    near = swap(mine, "grp", 1, grp_count)
    far = swap(mine, "grp", 2, grp_count)
    cut = cc * depth // 2
    corner = jnp.concatenate([swap(near[:, :cut], "grp", 2, grp_count), swap(far[:, cut:], "grp", 1, grp_count)], axis=1)
    lhs = [mine, near, far, corner]

    c_labels = lax.dynamic_slice_in_dim(irreps, chip * cc, cc, 0)
    a_labels = lax.dynamic_slice_in_dim(irreps, group * a_local, a_local, 0)
    pair_c = jnp.bitwise_xor(c_labels[:, None], irreps[None, :]).astype(jnp.bfloat16)
    pair_a = jnp.bitwise_xor(a_labels[:, None], irreps[None, :]).reshape(-1).astype(jnp.bfloat16)
    row_labels = jnp.broadcast_to(pair_c[:, :, None], (cc, nv, LANES))
    steps = -(-width // TILE_N)
    col_labels = jnp.full((1, steps * TILE_N), -1, jnp.bfloat16).at[0, :width].set(pair_a)
    col_labels = jnp.broadcast_to(col_labels, (16, steps * TILE_N))

    rows = grp_count * chips * per_device
    block = grp_count * per_device
    coded_width = round_up(width, LANES)
    where = jnp.stack([group, chip, core]).astype(jnp.int32)
    whole = lambda shape: pl.BlockSpec(shape, lambda i: (0,) * len(shape))
    codes, own = pl.pallas_call(
        lambda *refs: partial_kernel((grp_count, chips, cc, nv, width), *refs),
        grid=(steps,),
        in_specs=[pl.BlockSpec(memory_space=pltpu.SMEM)]
        + [whole((chips * per_device, cc * depth))] * grp_count
        + [pl.BlockSpec((half, nv, TILE_N), lambda i: (0, 0, i))] * 2
        + [whole((cc, nv, LANES)), pl.BlockSpec((16, TILE_N), lambda i: (0, i))],
        out_specs=[
            pl.BlockSpec((chips, block, TILE_N), lambda i: (0, 0, i)),
            pl.BlockSpec((block, TILE_N), lambda i: (0, i)),
        ],
        out_shape=[
            jax.ShapeDtypeStruct((chips, block, coded_width), jnp.int16),
            jax.ShapeDtypeStruct((block, width), jnp.float32),
        ],
        scratch_shapes=[
            pltpu.VMEM((rows, cc * depth), jnp.float32),
            pltpu.VMEM((rows, cc * depth), jnp.bfloat16),
            pltpu.VMEM((cc, depth, TILE_N), jnp.bfloat16),
            pltpu.VMEM((rows, LANES), jnp.float32),
        ],
        compiler_params=pltpu.CompilerParams(vmem_limit_bytes=60 * 2**20),
    )(where, *lhs, vvvv.reshape(half, nv, width), other.reshape(half, nv, width), row_labels, col_labels)

    arrived = [swap(codes[r], "mem", 2 * r, mem_count) for r in range(1, chips)]
    return pl.pallas_call(
        lambda *refs: combine_kernel(width, *refs),
        out_shape=jax.ShapeDtypeStruct((block, width), jnp.float32),
        compiler_params=pltpu.CompilerParams(vmem_limit_bytes=32 * 2**20),
    )(own, *arrived)


def solution(mesh):
    in_specs = (P(("grp", "mem"), None, None), P("mem", "grp"), P())
    out_specs = P("mem", "grp")
    return jax.shard_map(shards, mesh=mesh, in_specs=in_specs, out_specs=out_specs, check_vma=False)
```

```python
import jax
import jax.numpy as jnp
from jax import lax
from jax.experimental import pallas as pl
from jax.experimental.pallas import tpu as pltpu
from jax.sharding import PartitionSpec as P

LANES = 128
TILE_N = 512
QMAX = 32000.0
STEPS = 8.0
VMEM = pl.BlockSpec(memory_space=pltpu.VMEM)
SMEM = pl.BlockSpec(memory_space=pltpu.SMEM)


def round_up(value, unit):
    return -(-value // unit) * unit


def mask_kernel(base, where_ref, irreps_ref, row_ref, v_ref, out_ref, labels, held_left, held_right, sems):
    nv, width = v_ref.shape[1:]
    count, depth, padded = out_ref.shape
    middle = round_up(width // 2, LANES)
    spans = [(c, low, high) for c in range(count) for low, high in ((0, middle), (middle, width))]

    def fetch(i):
        c, low, high = spans[i]
        return pltpu.make_async_copy(v_ref.at[base + c, :, low:high], held(i).at[c], sems.at[i])

    def held(i):
        return held_left if i % 2 == 0 else held_right

    for i in range(len(spans)):
        fetch(i).start()
    row = row_ref[...]
    wide = jnp.concatenate([row, jnp.zeros((1, depth - nv), jnp.int32)], axis=1)
    labels[...] = jnp.broadcast_to(wide, (LANES, depth)).T
    first_a = where_ref[1]
    columns = jnp.concatenate([jnp.bitwise_xor(row, irreps_ref[first_a + a]) for a in range(width // nv)], axis=1)
    columns = columns.astype(jnp.bfloat16)
    for i, (c, low, high) in enumerate(spans):
        rows = jnp.bitwise_xor(labels[0:nv, :], irreps_ref[where_ref[0] + c]).astype(jnp.bfloat16)
        if low == 0:
            out_ref[c, nv:depth, :] = jnp.zeros((depth - nv, padded), jnp.bfloat16)
        fetch(i).wait()
        for n in range(low, high, LANES):
            end = min(n + LANES, high)
            keep = rows[:, 0:end - n] == columns[:, n:end]
            block = jnp.where(keep, held(i)[c, :, n - low:end - low], jnp.zeros((), jnp.bfloat16))
            if end < n + LANES:
                block = jnp.concatenate([block, jnp.zeros((nv, n + LANES - end), jnp.bfloat16)], axis=1)
            out_ref[c, 0:nv, n:n + LANES] = block


def dot_kernel(grp_count, where_ref, *refs):
    lhs_refs, part_refs = refs[:grp_count], refs[grp_count:-3]
    out_ref, wide, lhs = refs[-3:]
    group, chip = where_ref[0], where_ref[1]
    rows_each = lhs_refs[0].shape[0]
    per_group = where_ref.shape[0] - 2
    block = rows_each // per_group
    for j in range(grp_count):
        for q in range(per_group):
            at = jnp.bitwise_xor(jnp.bitwise_xor(group, j) * per_group + q, chip)
            rows = lhs_refs[j][q * block:(q + 1) * block, :].astype(jnp.float32)
            wide[pl.ds(pl.multiple_of(at * block, 8), block), :] = rows
    lhs[...] = wide[...].astype(jnp.bfloat16)
    padded = out_ref.shape[1]
    size = part_refs[0].shape[0] * part_refs[0].shape[1]
    for first in range(0, padded, TILE_N):
        last = min(first + TILE_N, padded)
        total = None
        for i, part_ref in enumerate(part_refs):
            right = part_ref[:, :, first:last].reshape(size, last - first)
            term = jnp.dot(lhs[:, i * size:(i + 1) * size], right, preferred_element_type=jnp.float32)
            total = term if total is None else total + term
        out_ref[:, first:last] = total


def code_kernel(width, mine_ref, theirs_ref, own_ref, *code_refs):
    count, padded = mine_ref.shape
    block = own_ref.shape[0]
    lane = lax.broadcasted_iota(jnp.int32, (count, LANES), 1)
    spare = width % LANES
    exponents = jnp.zeros((count, LANES), jnp.float32)
    for n in range(0, padded, LANES):
        part = mine_ref[:, n:n + LANES] + theirs_ref[:, n:n + LANES]
        own_ref[:, n:n + LANES] = part[:block]
        top = jnp.maximum(jnp.max(jnp.abs(part), axis=1, keepdims=True), 1e-30)
        level = jnp.ceil(jnp.log2(top) * STEPS + 0.05)
        code = jnp.round(part * (jnp.exp2(level * (-1.0 / STEPS)) * QMAX))
        exponents = jnp.where(lane == spare + n // LANES, level, exponents)
        if n + LANES == padded:
            code = jnp.where(lane >= spare, exponents, code)
        code = code.astype(jnp.int16)
        for r, code_ref in enumerate(code_refs, 1):
            code_ref[:, n:n + LANES] = code[r * block:(r + 1) * block]


def combine_kernel(width, own_ref, *refs):
    code_refs, out_ref = refs[:-1], refs[-1]
    base = width // LANES * LANES
    exponents = [jnp.exp2(ref[:, base:base + LANES].astype(jnp.float32) * (1.0 / STEPS)) * (1.0 / QMAX) for ref in code_refs]
    for low in range(0, width, LANES):
        high = min(low + LANES, width)
        at = width % LANES + low // LANES
        value = own_ref[:, low:high]
        for scale, ref in zip(exponents, code_refs):
            value = value + ref[:, low:high].astype(jnp.float32) * scale[:, at:at + 1]
        out_ref[:, low:high] = value


def shards(t_amps, vvvv, irreps):
    mem_count = lax.axis_size("mem")
    grp_count = lax.axis_size("grp")
    per_device, cw, nv = t_amps.shape
    chips = mem_count // 2
    cc = cw // chips
    half = cc // 2
    width = vvvv.shape[1]
    padded = round_up(width, LANES)
    depth = round_up(nv, LANES)
    a_local = width // nv
    mem = lax.axis_index("mem")
    group = lax.axis_index("grp")
    chip, core = mem // 2, mem % 2

    def swap(x, axis, k, count):
        return lax.ppermute(x, axis, [(i, i ^ k) for i in range(count)])

    hop = grp_count // 2

    def mask(source, owner, base, count):
        where = jnp.stack([owner * half + base, group * a_local]).astype(jnp.int32)
        blocks = pltpu.with_memory_space_constraint(source.reshape(half, nv, width), pltpu.HBM)
        return pl.pallas_call(
            lambda *refs: mask_kernel(base, *refs),
            in_specs=[SMEM, SMEM, VMEM, pl.BlockSpec(memory_space=pl.ANY)],
            out_specs=VMEM,
            out_shape=jax.ShapeDtypeStruct((count, depth, padded), jnp.bfloat16),
            scratch_shapes=[
                pltpu.VMEM((depth, LANES), jnp.int32),
                pltpu.VMEM((count, nv, round_up(width // 2, LANES)), jnp.bfloat16),
                pltpu.VMEM((count, nv, width - round_up(width // 2, LANES)), jnp.bfloat16),
                pltpu.SemaphoreType.DMA((2 * count,)),
            ],
            compiler_params=pltpu.CompilerParams(vmem_limit_bytes=16 * 2**20),
            cost_estimate=pl.CostEstimate(flops=0, bytes_accessed=4 * count * nv * width, transcendentals=0),
        )(where, irreps, irreps.reshape(1, nv), blocks)

    split = half // 2
    raw = t_amps.reshape(per_device, chips, 2, half, nv)
    kept = lax.dynamic_index_in_dim(raw, core, 2, keepdims=False)
    lent = swap(lax.dynamic_index_in_dim(raw, 1 - core, 2, keepdims=False), "mem", 1, mem_count)
    even = core == 0
    both = jnp.concatenate([jnp.where(even, kept, lent), jnp.where(even, lent, kept)])
    taken = [lax.dynamic_index_in_dim(both, jnp.bitwise_xor(chip, r), 1, keepdims=False) for r in range(chips)]
    got = [taken[0]] + [swap(taken[r], "mem", 2 * r, mem_count) for r in range(1, chips)]

    def beside(x):
        return [swap(x, "grp", 1, grp_count), swap(x, "grp", 2, grp_count)]

    def corner(near, far):
        cut = near.shape[0] // 2
        return jnp.concatenate([swap(near[:cut], "grp", 2, grp_count), swap(far[cut:], "grp", 1, grp_count)])

    x = jnp.concatenate(got[:chips // 2])
    y = jnp.concatenate(got[chips // 2:])
    x, late = lax.optimization_barrier((x, vvvv))
    x_beside = beside(x)
    parts = [mask(late, mem, 0, half)]
    x_beside, parts = lax.optimization_barrier((x_beside, parts))
    x_corner = corner(*x_beside)
    y_beside = beside(y)
    halves = [[x] + x_beside + [x_corner], [y] + y_beside + [corner(*y_beside)]]

    pair_rows = 2 * per_device
    kept_lhs, lent_lhs = [], []
    for one, two in zip(*halves):
        stack = jnp.concatenate([one, two]).reshape(chips, pair_rows, half, nv)
        stack = [stack[j] for j in range(chips)]
        bit = 1
        while bit < chips:
            flip = jnp.bitwise_and(chip, bit) != 0
            stack = [jnp.where(flip, stack[j ^ bit], stack[j]) for j in range(chips)]
            bit *= 2
        for lhs, target in ((kept_lhs, core), (lent_lhs, 1 - core)):
            first = target == 0
            rows = [jnp.where(first, stack[j], stack[j + hop]) for j in range(chips) if j // hop % 2 == 0]
            filled = jnp.pad(jnp.concatenate(rows), ((0, 0), (0, 0), (0, depth - nv)))
            lhs.append(filled.reshape(chips // 2 * pair_rows, half * depth))

    rows = grp_count * chips // 2 * pair_rows
    block = hop * pair_rows
    where = jnp.stack([group, chip] + [0] * (chips // grp_count)).astype(jnp.int32)

    def multiply(lhs):
        return pl.pallas_call(
            lambda *refs: dot_kernel(grp_count, *refs),
            in_specs=[SMEM] + [VMEM] * (grp_count + len(parts)),
            out_specs=VMEM,
            out_shape=jax.ShapeDtypeStruct((rows, padded), jnp.float32),
            scratch_shapes=[
                pltpu.VMEM((rows, half * depth), jnp.float32),
                pltpu.VMEM((rows, half * depth), jnp.bfloat16),
            ],
            compiler_params=pltpu.CompilerParams(vmem_limit_bytes=round_up(rows * half * depth * 6, 2**20) + 6 * 2**20),
            cost_estimate=pl.CostEstimate(flops=2 * rows * half * nv * width, bytes_accessed=4 * rows * width, transcendentals=0),
        )(where, *lhs, *parts)

    theirs = swap(multiply(lent_lhs), "mem", 1, mem_count)
    outs = pl.pallas_call(
        lambda *refs: code_kernel(width, *refs),
        in_specs=[VMEM] * 2,
        out_specs=[VMEM] * chips,
        out_shape=[jax.ShapeDtypeStruct((block, padded), jnp.float32)]
        + [jax.ShapeDtypeStruct((block, padded), jnp.int16)] * (chips - 1),
        compiler_params=pltpu.CompilerParams(vmem_limit_bytes=16 * 2**20),
    )(multiply(kept_lhs), theirs)

    arrived = [swap(outs[r], "mem", 2 * r, mem_count) for r in range(1, chips)]
    return pl.pallas_call(
        lambda *refs: combine_kernel(width, *refs),
        out_shape=jax.ShapeDtypeStruct((block, width), jnp.float32),
        compiler_params=pltpu.CompilerParams(vmem_limit_bytes=8 * 2**20),
    )(outs[0], *arrived)


def solution(mesh):
    in_specs = (P(("grp", "mem"), None, None), P("mem", "grp"), P())
    out_specs = P("mem", "grp")
    return jax.shard_map(shards, mesh=mesh, in_specs=in_specs, out_specs=out_specs, check_vma=False)
```

```python
import jax
import jax.numpy as jnp
from jax import lax
from jax.experimental import pallas as pl
from jax.experimental.pallas import tpu as pltpu
from jax.sharding import PartitionSpec as P

LANES = 128
TILE_N = 512
QMAX = 32000.0
STEPS = 8.0
VMEM = pl.BlockSpec(memory_space=pltpu.VMEM)
SMEM = pl.BlockSpec(memory_space=pltpu.SMEM)


def round_up(value, unit):
    return -(-value // unit) * unit


def mask_kernel(base, where_ref, irreps_ref, row_ref, v_ref, out_ref, labels, held_left, held_right, sems):
    nv, width = v_ref.shape[1:]
    count, depth, padded = out_ref.shape
    middle = round_up(width // 2, LANES)
    spans = [(c, low, high) for c in range(count) for low, high in ((0, middle), (middle, width))]

    def fetch(i):
        c, low, high = spans[i]
        return pltpu.make_async_copy(v_ref.at[base + c, :, low:high], held(i).at[c], sems.at[i])

    def held(i):
        return held_left if i % 2 == 0 else held_right

    for i in range(len(spans)):
        fetch(i).start()
    row = row_ref[...]
    wide = jnp.concatenate([row, jnp.zeros((1, depth - nv), jnp.int32)], axis=1)
    labels[...] = jnp.broadcast_to(wide, (LANES, depth)).T
    first_a = where_ref[1]
    columns = jnp.concatenate([jnp.bitwise_xor(row, irreps_ref[first_a + a]) for a in range(width // nv)], axis=1)
    columns = columns.astype(jnp.bfloat16)
    for i, (c, low, high) in enumerate(spans):
        rows = jnp.bitwise_xor(labels[0:nv, :], irreps_ref[where_ref[0] + c]).astype(jnp.bfloat16)
        if low == 0:
            out_ref[c, nv:depth, :] = jnp.zeros((depth - nv, padded), jnp.bfloat16)
        fetch(i).wait()
        for n in range(low, high, LANES):
            end = min(n + LANES, high)
            keep = rows[:, 0:end - n] == columns[:, n:end]
            block = jnp.where(keep, held(i)[c, :, n - low:end - low], jnp.zeros((), jnp.bfloat16))
            if end < n + LANES:
                block = jnp.concatenate([block, jnp.zeros((nv, n + LANES - end), jnp.bfloat16)], axis=1)
            out_ref[c, 0:nv, n:n + LANES] = block


def dot_kernel(grp_count, where_ref, *refs):
    lhs_refs, part_refs = refs[:grp_count], refs[grp_count:-3]
    out_ref, wide, lhs = refs[-3:]
    group, chip = where_ref[0], where_ref[1]
    rows_each = lhs_refs[0].shape[0]
    per_group = where_ref.shape[0] - 2
    block = rows_each // per_group
    for j in range(grp_count):
        for q in range(per_group):
            at = jnp.bitwise_xor(jnp.bitwise_xor(group, j) * per_group + q, chip)
            rows = lhs_refs[j][q * block:(q + 1) * block, :].astype(jnp.float32)
            wide[pl.ds(pl.multiple_of(at * block, 8), block), :] = rows
    lhs[...] = wide[...].astype(jnp.bfloat16)
    padded = out_ref.shape[1]
    size = part_refs[0].shape[0] * part_refs[0].shape[1]
    for first in range(0, padded, TILE_N):
        last = min(first + TILE_N, padded)
        total = None
        for i, part_ref in enumerate(part_refs):
            right = part_ref[:, :, first:last].reshape(size, last - first)
            term = jnp.dot(lhs[:, i * size:(i + 1) * size], right, preferred_element_type=jnp.float32)
            total = term if total is None else total + term
        out_ref[:, first:last] = total


def encode(part, lane, at, exponents):
    top = jnp.maximum(jnp.max(jnp.abs(part), axis=1, keepdims=True), 1e-30)
    level = jnp.ceil(jnp.log2(top) * STEPS + 0.05)
    code = jnp.round(part * (jnp.exp2(level * (-1.0 / STEPS)) * QMAX))
    return code, jnp.where(lane == at, level, exponents)


def scale_of(ref):
    last = ref[:, ref.shape[1] - LANES:].astype(jnp.float32)
    return jnp.exp2(last * (1.0 / STEPS)) * (1.0 / QMAX)


def code_kernel(width, split, mine_ref, theirs_ref, own_ref, next_ref, *refs):
    count, padded = mine_ref.shape
    block = own_ref.shape[0]
    chips = count // block
    low_refs, high_refs = refs[:chips - 2], refs[chips - 2:]
    lane = lax.broadcasted_iota(jnp.int32, (count, LANES), 1)
    spare = width % LANES
    exponents = jnp.zeros((count, LANES), jnp.float32)
    for n in range(0, padded, LANES):
        part = mine_ref[:, n:n + LANES] + theirs_ref[:, n:n + LANES]
        own_ref[:, n:n + LANES] = part[:block]
        code, exponents = encode(part, lane, spare + n // LANES, exponents)
        if n + LANES == padded:
            code = jnp.where(lane >= spare, exponents, code)
        code = code.astype(jnp.int16)
        next_ref[:, n:n + LANES] = code[block:2 * block]
        for r in range(2, chips):
            rows = slice(r * block, (r + 1) * block)
            if n < split:
                low_refs[r - 2][:, n:n + LANES] = code[rows]
            elif r % 2 == 0:
                high_refs[r - 2][:, n - split:n - split + LANES] = part[rows]
            else:
                high_refs[r - 2][:, n - split:n - split + LANES] = code[rows]
    exponents = exponents.astype(jnp.int16)
    for r in range(2, chips):
        low_refs[r - 2][:, split:split + LANES] = exponents[r * block:(r + 1) * block]


def relay_kernel(width, split, *refs):
    count = len(refs) // 3
    spare = width % LANES
    for mine_ref, code_ref, out_ref in zip(refs[:count], refs[count:2 * count], refs[2 * count:]):
        block, size = mine_ref.shape
        lane = lax.broadcasted_iota(jnp.int32, (block, LANES), 1)
        scale = scale_of(code_ref)
        exponents = jnp.zeros((block, LANES), jnp.float32)
        for n in range(0, size, LANES):
            at = spare + (n + split) // LANES
            part = mine_ref[:, n:n + LANES] + code_ref[:, n:n + LANES].astype(jnp.float32) * scale[:, at:at + 1]
            if n + LANES == size:
                part = jnp.where(lane < spare, part, 0.0)
            code, exponents = encode(part, lane, at, exponents)
            if n + LANES == size:
                code = jnp.where(lane >= spare, exponents, code)
            out_ref[:, n:n + LANES] = code.astype(jnp.int16)


def combine_kernel(width, split, own_ref, next_ref, *refs):
    out_ref = refs[-1]
    cut = 2 * (len(refs) - 1) // 3
    lows, highs = refs[:cut], refs[cut:-1]
    next_scale = scale_of(next_ref)
    low_scales = [scale_of(ref) for ref in lows]
    high_scales = [scale_of(ref) for ref in highs]
    for low in range(0, width, LANES):
        high = min(low + LANES, width)
        at = width % LANES + low // LANES
        value = own_ref[:, low:high] + next_ref[:, low:high].astype(jnp.float32) * next_scale[:, at:at + 1]
        some, scales, base = (lows, low_scales, 0) if low < split else (highs, high_scales, split)
        for scale, ref in zip(scales, some):
            value = value + ref[:, low - base:high - base].astype(jnp.float32) * scale[:, at:at + 1]
        out_ref[:, low:high] = value


def shards(t_amps, vvvv, irreps):
    mem_count = lax.axis_size("mem")
    grp_count = lax.axis_size("grp")
    per_device, cw, nv = t_amps.shape
    chips = mem_count // 2
    cc = cw // chips
    half = cc // 2
    width = vvvv.shape[1]
    padded = round_up(width, LANES)
    depth = round_up(nv, LANES)
    a_local = width // nv
    mem = lax.axis_index("mem")
    group = lax.axis_index("grp")
    chip, core = mem // 2, mem % 2

    def swap(x, axis, k, count):
        return lax.ppermute(x, axis, [(i, i ^ k) for i in range(count)])

    hop = grp_count // 2

    def mask(source, owner, base, count):
        where = jnp.stack([owner * half + base, group * a_local]).astype(jnp.int32)
        blocks = pltpu.with_memory_space_constraint(source.reshape(half, nv, width), pltpu.HBM)
        return pl.pallas_call(
            lambda *refs: mask_kernel(base, *refs),
            in_specs=[SMEM, SMEM, VMEM, pl.BlockSpec(memory_space=pl.ANY)],
            out_specs=VMEM,
            out_shape=jax.ShapeDtypeStruct((count, depth, padded), jnp.bfloat16),
            scratch_shapes=[
                pltpu.VMEM((depth, LANES), jnp.int32),
                pltpu.VMEM((count, nv, round_up(width // 2, LANES)), jnp.bfloat16),
                pltpu.VMEM((count, nv, width - round_up(width // 2, LANES)), jnp.bfloat16),
                pltpu.SemaphoreType.DMA((2 * count,)),
            ],
            compiler_params=pltpu.CompilerParams(vmem_limit_bytes=16 * 2**20),
            cost_estimate=pl.CostEstimate(flops=0, bytes_accessed=4 * count * nv * width, transcendentals=0),
        )(where, irreps, irreps.reshape(1, nv), blocks)

    split = half // 2
    raw = t_amps.reshape(per_device, chips, 2, half, nv)
    kept = lax.dynamic_index_in_dim(raw, core, 2, keepdims=False)
    lent = swap(lax.dynamic_index_in_dim(raw, 1 - core, 2, keepdims=False), "mem", 1, mem_count)
    even = core == 0
    both = jnp.concatenate([jnp.where(even, kept, lent), jnp.where(even, lent, kept)])
    taken = [lax.dynamic_index_in_dim(both, jnp.bitwise_xor(chip, r), 1, keepdims=False) for r in range(chips)]
    got = [taken[0]] + [swap(taken[r], "mem", 2 * r, mem_count) for r in range(1, chips)]

    def beside(x):
        return [swap(x, "grp", 1, grp_count), swap(x, "grp", 2, grp_count)]

    def corner(near, far):
        cut = near.shape[0] // 2
        return jnp.concatenate([swap(near[:cut], "grp", 2, grp_count), swap(far[cut:], "grp", 1, grp_count)])

    def around(x):
        return [x] + [swap(x, "grp", k, grp_count) for k in range(1, grp_count)]

    x = jnp.concatenate(got[:chips // 2])
    y = jnp.concatenate(got[chips // 2:])
    x_all = around(x)
    y, late = lax.optimization_barrier((y, vvvv))
    parts = [mask(late, mem, 0, half // 2)]
    x_all, parts, late = lax.optimization_barrier((x_all, parts, late))
    y_all, part = lax.optimization_barrier((around(y), mask(late, mem, half // 2, half // 2)))
    parts.append(part)
    halves = [x_all, y_all]

    pair_rows = 2 * per_device
    kept_lhs, lent_lhs = [], []
    for one, two in zip(*halves):
        stack = jnp.concatenate([one, two]).reshape(chips, pair_rows, half, nv)
        stack = [stack[j] for j in range(chips)]
        bit = 1
        while bit < chips:
            flip = jnp.bitwise_and(chip, bit) != 0
            stack = [jnp.where(flip, stack[j ^ bit], stack[j]) for j in range(chips)]
            bit *= 2
        for lhs, target in ((kept_lhs, core), (lent_lhs, 1 - core)):
            first = target == 0
            rows = [jnp.where(first, stack[j], stack[j + hop]) for j in range(chips) if j // hop % 2 == 0]
            filled = jnp.pad(jnp.concatenate(rows), ((0, 0), (0, 0), (0, depth - nv)))
            lhs.append(filled.reshape(chips // 2 * pair_rows, half * depth))

    rows = grp_count * chips // 2 * pair_rows
    block = hop * pair_rows
    where = jnp.stack([group, chip] + [0] * (chips // grp_count)).astype(jnp.int32)

    def multiply(lhs):
        return pl.pallas_call(
            lambda *refs: dot_kernel(grp_count, *refs),
            in_specs=[SMEM] + [VMEM] * (grp_count + len(parts)),
            out_specs=VMEM,
            out_shape=jax.ShapeDtypeStruct((rows, padded), jnp.float32),
            scratch_shapes=[
                pltpu.VMEM((rows, half * depth), jnp.float32),
                pltpu.VMEM((rows, half * depth), jnp.bfloat16),
            ],
            compiler_params=pltpu.CompilerParams(vmem_limit_bytes=round_up(rows * half * depth * 6, 2**20) + 6 * 2**20),
            cost_estimate=pl.CostEstimate(flops=2 * rows * half * nv * width, bytes_accessed=4 * rows * width, transcendentals=0),
        )(where, *lhs, *parts)

    theirs = swap(multiply(lent_lhs), "mem", 1, mem_count)
    split = padded // LANES // 2 * LANES
    far_rounds = range(2, chips)
    outs = pl.pallas_call(
        lambda *refs: code_kernel(width, split, *refs),
        in_specs=[VMEM] * 2,
        out_specs=[VMEM] * (2 + 2 * len(far_rounds)),
        out_shape=[
            jax.ShapeDtypeStruct((block, padded), jnp.float32),
            jax.ShapeDtypeStruct((block, padded), jnp.int16),
        ]
        + [jax.ShapeDtypeStruct((block, split + LANES), jnp.int16) for r in far_rounds]
        + [jax.ShapeDtypeStruct((block, padded - split), jnp.int16 if r % 2 else jnp.float32) for r in far_rounds],
        compiler_params=pltpu.CompilerParams(vmem_limit_bytes=16 * 2**20),
    )(multiply(kept_lhs), theirs)
    own, beside_code = outs[:2]
    lows = dict(zip(far_rounds, outs[2:]))
    highs = dict(zip(far_rounds, outs[2 + len(far_rounds):]))
    evens = [r for r in far_rounds if r % 2 == 0]

    helped = [swap(highs[r + 1], "mem", 2, mem_count) for r in evens]
    arrived = [swap(lows[r], "mem", 2 * r, mem_count) for r in far_rounds]
    near_arrived = swap(beside_code, "mem", 2, mem_count)
    relayed = pl.pallas_call(
        lambda *refs: relay_kernel(width, split, *refs),
        in_specs=[VMEM] * (2 * len(evens)),
        out_specs=[VMEM] * len(evens),
        out_shape=[jax.ShapeDtypeStruct((block, padded - split), jnp.int16)] * len(evens),
        compiler_params=pltpu.CompilerParams(vmem_limit_bytes=8 * 2**20),
    )(*[highs[r] for r in evens], *helped)
    high_arrived = [swap(relayed[i], "mem", 2 * r, mem_count) for i, r in enumerate(evens)]
    return pl.pallas_call(
        lambda *refs: combine_kernel(width, split, *refs),
        in_specs=[VMEM] * (2 + len(far_rounds) + len(evens)),
        out_specs=VMEM,
        out_shape=jax.ShapeDtypeStruct((block, width), jnp.float32),
        compiler_params=pltpu.CompilerParams(vmem_limit_bytes=8 * 2**20),
    )(own, near_arrived, *arrived, *high_arrived)


def solution(mesh):
    in_specs = (P(("grp", "mem"), None, None), P("mem", "grp"), P())
    out_specs = P("mem", "grp")
    return jax.shard_map(shards, mesh=mesh, in_specs=in_specs, out_specs=out_specs, check_vma=False)
```

```python
import jax
import jax.numpy as jnp
from jax import lax
from jax.experimental import pallas as pl
from jax.experimental.pallas import tpu as pltpu
from jax.sharding import PartitionSpec as P

LANES = 128
TILE_N = 512
QMAX = 32000.0
STEPS = 8.0
VMEM = pl.BlockSpec(memory_space=pltpu.VMEM)
SMEM = pl.BlockSpec(memory_space=pltpu.SMEM)


def round_up(value, unit):
    return -(-value // unit) * unit


def mask_kernel(base, where_ref, irreps_ref, row_ref, v_ref, out_ref, labels, held_left, held_right, sems):
    nv, width = v_ref.shape[1:]
    count, depth, padded = out_ref.shape
    middle = round_up(width // 2, LANES)
    spans = [(c, low, high) for c in range(count) for low, high in ((0, middle), (middle, width))]

    def fetch(i):
        c, low, high = spans[i]
        return pltpu.make_async_copy(v_ref.at[base + c, :, low:high], held(i).at[c], sems.at[i])

    def held(i):
        return held_left if i % 2 == 0 else held_right

    for i in range(len(spans)):
        fetch(i).start()
    row = row_ref[...]
    wide = jnp.concatenate([row, jnp.zeros((1, depth - nv), jnp.int32)], axis=1)
    labels[...] = jnp.broadcast_to(wide, (LANES, depth)).T
    first_a = where_ref[1]
    columns = jnp.concatenate([jnp.bitwise_xor(row, irreps_ref[first_a + a]) for a in range(width // nv)], axis=1)
    columns = columns.astype(jnp.bfloat16)
    for i, (c, low, high) in enumerate(spans):
        rows = jnp.bitwise_xor(labels[0:nv, :], irreps_ref[where_ref[0] + c]).astype(jnp.bfloat16)
        if low == 0:
            out_ref[c, nv:depth, :] = jnp.zeros((depth - nv, padded), jnp.bfloat16)
        fetch(i).wait()
        for n in range(low, high, LANES):
            end = min(n + LANES, high)
            keep = rows[:, 0:end - n] == columns[:, n:end]
            block = jnp.where(keep, held(i)[c, :, n - low:end - low], jnp.zeros((), jnp.bfloat16))
            if end < n + LANES:
                block = jnp.concatenate([block, jnp.zeros((nv, n + LANES - end), jnp.bfloat16)], axis=1)
            out_ref[c, 0:nv, n:n + LANES] = block


def dot_kernel(grp_count, where_ref, *refs):
    lhs_refs, part_refs = refs[:grp_count], refs[grp_count:-2]
    out_ref, lhs = refs[-2:]
    group, chip = where_ref[0], where_ref[1]
    rows_each = lhs_refs[0].shape[0]
    per_group = where_ref.shape[0] - 2
    block = rows_each // per_group
    places = []
    for j in range(grp_count):
        lhs[j * rows_each:(j + 1) * rows_each, :] = lhs_refs[j][...]
        for q in range(per_group):
            at = jnp.bitwise_xor(jnp.bitwise_xor(group, j) * per_group + q, chip)
            places.append(pl.ds(pl.multiple_of(at * block, 8), block))
    padded = out_ref.shape[1]
    size = part_refs[0].shape[0] * part_refs[0].shape[1]
    for first in range(0, padded, TILE_N):
        last = min(first + TILE_N, padded)
        total = None
        for i, part_ref in enumerate(part_refs):
            right = part_ref[:, :, first:last].reshape(size, last - first)
            term = jnp.dot(lhs[:, i * size:(i + 1) * size], right, preferred_element_type=jnp.float32)
            total = term if total is None else total + term
        for i, rows in enumerate(places):
            out_ref[rows, first:last] = total[i * block:(i + 1) * block]


def encode(part, lane, at, exponents):
    top = jnp.maximum(jnp.max(jnp.abs(part), axis=1, keepdims=True), 1e-30)
    level = jnp.ceil(jnp.log2(top) * STEPS + 0.05)
    code = jnp.round(part * (jnp.exp2(level * (-1.0 / STEPS)) * QMAX))
    return code, jnp.where(lane == at, level, exponents)


def scale_of(ref):
    last = ref[:, ref.shape[1] - LANES:].astype(jnp.float32)
    return jnp.exp2(last * (1.0 / STEPS)) * (1.0 / QMAX)


def code_kernel(width, split, mine_ref, theirs_ref, own_ref, next_ref, *refs):
    count, padded = mine_ref.shape
    block = own_ref.shape[0]
    chips = count // block
    low_refs, high_refs = refs[:chips - 2], refs[chips - 2:]
    lane = lax.broadcasted_iota(jnp.int32, (count, LANES), 1)
    spare = width % LANES
    exponents = jnp.zeros((count, LANES), jnp.float32)
    for n in range(0, padded, LANES):
        part = mine_ref[:, n:n + LANES] + theirs_ref[:, n:n + LANES]
        own_ref[:, n:n + LANES] = part[:block]
        code, exponents = encode(part, lane, spare + n // LANES, exponents)
        if n + LANES == padded:
            code = jnp.where(lane >= spare, exponents, code)
        code = code.astype(jnp.int16)
        next_ref[:, n:n + LANES] = code[block:2 * block]
        for r in range(2, chips):
            rows = slice(r * block, (r + 1) * block)
            if n < split:
                low_refs[r - 2][:, n:n + LANES] = code[rows]
            elif r % 2 == 0:
                high_refs[r - 2][:, n - split:n - split + LANES] = part[rows]
            else:
                high_refs[r - 2][:, n - split:n - split + LANES] = code[rows]
    exponents = exponents.astype(jnp.int16)
    for r in range(2, chips):
        low_refs[r - 2][:, split:split + LANES] = exponents[r * block:(r + 1) * block]


def relay_kernel(width, split, *refs):
    count = len(refs) // 3
    spare = width % LANES
    for mine_ref, code_ref, out_ref in zip(refs[:count], refs[count:2 * count], refs[2 * count:]):
        block, size = mine_ref.shape
        lane = lax.broadcasted_iota(jnp.int32, (block, LANES), 1)
        scale = scale_of(code_ref)
        exponents = jnp.zeros((block, LANES), jnp.float32)
        for n in range(0, size, LANES):
            at = spare + (n + split) // LANES
            part = mine_ref[:, n:n + LANES] + code_ref[:, n:n + LANES].astype(jnp.float32) * scale[:, at:at + 1]
            if n + LANES == size:
                part = jnp.where(lane < spare, part, 0.0)
            code, exponents = encode(part, lane, at, exponents)
            if n + LANES == size:
                code = jnp.where(lane >= spare, exponents, code)
            out_ref[:, n:n + LANES] = code.astype(jnp.int16)


def combine_kernel(width, split, own_ref, next_ref, *refs):
    out_ref = refs[-1]
    cut = 2 * (len(refs) - 1) // 3
    lows, highs = refs[:cut], refs[cut:-1]
    next_scale = scale_of(next_ref)
    low_scales = [scale_of(ref) for ref in lows]
    high_scales = [scale_of(ref) for ref in highs]
    for low in range(0, width, LANES):
        high = min(low + LANES, width)
        at = width % LANES + low // LANES
        value = own_ref[:, low:high] + next_ref[:, low:high].astype(jnp.float32) * next_scale[:, at:at + 1]
        some, scales, base = (lows, low_scales, 0) if low < split else (highs, high_scales, split)
        for scale, ref in zip(scales, some):
            value = value + ref[:, low - base:high - base].astype(jnp.float32) * scale[:, at:at + 1]
        out_ref[:, low:high] = value


def shards(t_amps, vvvv, irreps):
    mem_count = lax.axis_size("mem")
    grp_count = lax.axis_size("grp")
    per_device, cw, nv = t_amps.shape
    chips = mem_count // 2
    cc = cw // chips
    half = cc // 2
    width = vvvv.shape[1]
    padded = round_up(width, LANES)
    depth = round_up(nv, LANES)
    a_local = width // nv
    mem = lax.axis_index("mem")
    group = lax.axis_index("grp")
    chip, core = mem // 2, mem % 2

    def swap(x, axis, k, count):
        return lax.ppermute(x, axis, [(i, i ^ k) for i in range(count)])

    hop = grp_count // 2

    def mask(source, owner, base, count):
        where = jnp.stack([owner * half + base, group * a_local]).astype(jnp.int32)
        blocks = pltpu.with_memory_space_constraint(source.reshape(half, nv, width), pltpu.HBM)
        return pl.pallas_call(
            lambda *refs: mask_kernel(base, *refs),
            in_specs=[SMEM, SMEM, VMEM, pl.BlockSpec(memory_space=pl.ANY)],
            out_specs=VMEM,
            out_shape=jax.ShapeDtypeStruct((count, depth, padded), jnp.bfloat16),
            scratch_shapes=[
                pltpu.VMEM((depth, LANES), jnp.int32),
                pltpu.VMEM((count, nv, round_up(width // 2, LANES)), jnp.bfloat16),
                pltpu.VMEM((count, nv, width - round_up(width // 2, LANES)), jnp.bfloat16),
                pltpu.SemaphoreType.DMA((2 * count,)),
            ],
            compiler_params=pltpu.CompilerParams(vmem_limit_bytes=16 * 2**20),
            cost_estimate=pl.CostEstimate(flops=0, bytes_accessed=4 * count * nv * width, transcendentals=0),
        )(where, irreps, irreps.reshape(1, nv), blocks)

    split = half // 2
    raw = t_amps.reshape(per_device, chips, 2, half, nv)
    kept = lax.dynamic_index_in_dim(raw, core, 2, keepdims=False)
    lent = swap(lax.dynamic_index_in_dim(raw, 1 - core, 2, keepdims=False), "mem", 1, mem_count)
    even = core == 0
    both = jnp.concatenate([jnp.where(even, kept, lent), jnp.where(even, lent, kept)])
    taken = [lax.dynamic_index_in_dim(both, jnp.bitwise_xor(chip, r), 1, keepdims=False) for r in range(chips)]
    got = [taken[0]] + [swap(taken[r], "mem", 2 * r, mem_count) for r in range(1, chips)]

    def beside(x):
        return [swap(x, "grp", 1, grp_count), swap(x, "grp", 2, grp_count)]

    def corner(near, far):
        cut = near.shape[0] // 2
        return jnp.concatenate([swap(near[:cut], "grp", 2, grp_count), swap(far[cut:], "grp", 1, grp_count)])

    def around(x):
        return [x] + [swap(x, "grp", k, grp_count) for k in range(1, grp_count)]

    def in_order(some):
        bit = 1
        while bit < len(some):
            flip = jnp.bitwise_and(chip, bit) != 0
            some = [jnp.where(flip, some[j ^ bit], some[j]) for j in range(len(some))]
            bit *= 2
        return jnp.concatenate(some)

    x = in_order(got[:chips // 2])
    y = in_order(got[chips // 2:])
    x_all = around(x)
    y, late, x_all[3] = lax.optimization_barrier((y, vvvv, x_all[3]))
    parts = [mask(late, mem, 0, half // 2)]
    x_all, parts, late = lax.optimization_barrier((x_all, parts, late))
    y_all, part = lax.optimization_barrier((around(y), mask(late, mem, half // 2, half // 2)))
    parts.append(part)
    halves = [x_all, y_all]

    pair_rows = 2 * per_device
    kept_lhs, lent_lhs = [], []
    is_upper = chip // (chips // 2)
    for one, two in zip(*halves):
        for lhs, target in ((kept_lhs, core), (lent_lhs, 1 - core)):
            if chips // 2 == hop:
                rows = [jnp.where(is_upper == target, one, two)]
            else:
                near, far = [x.reshape(chips // 2, pair_rows, half, nv) for x in (one, two)]
                wanted = target == 0
                rows = []
                for upper in (0, 1):
                    stack = jnp.where(is_upper == upper, near, far)
                    rows += [jnp.where(wanted, stack[j], stack[j + hop]) for j in range(chips // 2) if j // hop % 2 == 0]
            filled = jnp.pad(jnp.concatenate(rows), ((0, 0), (0, 0), (0, depth - nv)))
            lhs.append(filled.reshape(chips // 2 * pair_rows, half * depth))

    rows = grp_count * chips // 2 * pair_rows
    block = hop * pair_rows
    where = jnp.stack([group, chip] + [0] * (chips // grp_count)).astype(jnp.int32)

    def multiply(lhs):
        return pl.pallas_call(
            lambda *refs: dot_kernel(grp_count, *refs),
            in_specs=[SMEM] + [VMEM] * (grp_count + len(parts)),
            out_specs=VMEM,
            out_shape=jax.ShapeDtypeStruct((rows, padded), jnp.float32),
            scratch_shapes=[pltpu.VMEM((rows, half * depth), jnp.bfloat16)],
            compiler_params=pltpu.CompilerParams(vmem_limit_bytes=round_up(rows * half * depth * 6, 2**20) + 6 * 2**20),
            cost_estimate=pl.CostEstimate(flops=2 * rows * half * nv * width, bytes_accessed=4 * rows * width, transcendentals=0),
        )(where, *lhs, *parts)

    theirs = swap(multiply(lent_lhs), "mem", 1, mem_count)
    split = padded // LANES // 2 * LANES
    far_rounds = range(2, chips)
    outs = pl.pallas_call(
        lambda *refs: code_kernel(width, split, *refs),
        in_specs=[VMEM] * 2,
        out_specs=[VMEM] * (2 + 2 * len(far_rounds)),
        out_shape=[
            jax.ShapeDtypeStruct((block, padded), jnp.float32),
            jax.ShapeDtypeStruct((block, padded), jnp.int16),
        ]
        + [jax.ShapeDtypeStruct((block, split + LANES), jnp.int16) for r in far_rounds]
        + [jax.ShapeDtypeStruct((block, padded - split), jnp.int16 if r % 2 else jnp.float32) for r in far_rounds],
        compiler_params=pltpu.CompilerParams(vmem_limit_bytes=16 * 2**20),
    )(multiply(kept_lhs), theirs)
    own, beside_code = outs[:2]
    lows = dict(zip(far_rounds, outs[2:]))
    highs = dict(zip(far_rounds, outs[2 + len(far_rounds):]))
    evens = [r for r in far_rounds if r % 2 == 0]

    helped = [swap(highs[r + 1], "mem", 2, mem_count) for r in evens]
    near_arrived = swap(beside_code, "mem", 2, mem_count)
    arrived = [swap(lows[r], "mem", 2 * r, mem_count) for r in far_rounds]
    relayed = pl.pallas_call(
        lambda *refs: relay_kernel(width, split, *refs),
        in_specs=[VMEM] * (2 * len(evens)),
        out_specs=[VMEM] * len(evens),
        out_shape=[jax.ShapeDtypeStruct((block, padded - split), jnp.int16)] * len(evens),
        compiler_params=pltpu.CompilerParams(vmem_limit_bytes=8 * 2**20),
    )(*[highs[r] for r in evens], *helped)
    high_arrived = [swap(relayed[i], "mem", 2 * r, mem_count) for i, r in enumerate(evens)]
    return pl.pallas_call(
        lambda *refs: combine_kernel(width, split, *refs),
        in_specs=[VMEM] * (2 + len(far_rounds) + len(evens)),
        out_specs=VMEM,
        out_shape=jax.ShapeDtypeStruct((block, width), jnp.float32),
        compiler_params=pltpu.CompilerParams(vmem_limit_bytes=8 * 2**20),
    )(own, near_arrived, *arrived, *high_arrived)


def solution(mesh):
    in_specs = (P(("grp", "mem"), None, None), P("mem", "grp"), P())
    out_specs = P("mem", "grp")
    return jax.shard_map(shards, mesh=mesh, in_specs=in_specs, out_specs=out_specs, check_vma=False)
```

```python
import jax
import jax.numpy as jnp
from jax import lax
from jax.experimental import pallas as pl
from jax.experimental.pallas import tpu as pltpu
from jax.sharding import PartitionSpec as P

LANES = 128
TILE_N = 512
QMAX = 32000.0
STEPS = 8.0
VMEM = pl.BlockSpec(memory_space=pltpu.VMEM)
SMEM = pl.BlockSpec(memory_space=pltpu.SMEM)


def round_up(value, unit):
    return -(-value // unit) * unit


def mask_kernel(base, where_ref, irreps_ref, row_ref, v_ref, out_ref, labels, held_left, held_right, sems):
    nv, width = v_ref.shape[1:]
    count, depth, padded = out_ref.shape
    middle = round_up(width // 2, LANES)
    spans = [(c, low, high) for c in range(count) for low, high in ((0, middle), (middle, width))]

    def fetch(i):
        c, low, high = spans[i]
        return pltpu.make_async_copy(v_ref.at[base + c, :, low:high], held(i).at[c], sems.at[i])

    def held(i):
        return held_left if i % 2 == 0 else held_right

    for i in range(len(spans)):
        fetch(i).start()
    row = row_ref[...]
    wide = jnp.concatenate([row, jnp.zeros((1, depth - nv), jnp.int32)], axis=1)
    labels[...] = jnp.broadcast_to(wide, (LANES, depth)).T
    first_a = where_ref[1]
    columns = jnp.concatenate([jnp.bitwise_xor(row, irreps_ref[first_a + a]) for a in range(width // nv)], axis=1)
    columns = columns.astype(jnp.bfloat16)
    for i, (c, low, high) in enumerate(spans):
        rows = jnp.bitwise_xor(labels[0:nv, :], irreps_ref[where_ref[0] + c]).astype(jnp.bfloat16)
        if low == 0:
            out_ref[c, nv:depth, :] = jnp.zeros((depth - nv, padded), jnp.bfloat16)
        fetch(i).wait()
        for n in range(low, high, LANES):
            end = min(n + LANES, high)
            keep = rows[:, 0:end - n] == columns[:, n:end]
            block = jnp.where(keep, held(i)[c, :, n - low:end - low], jnp.zeros((), jnp.bfloat16))
            if end < n + LANES:
                block = jnp.concatenate([block, jnp.zeros((nv, n + LANES - end), jnp.bfloat16)], axis=1)
            out_ref[c, 0:nv, n:n + LANES] = block


def dot_kernel(grp_count, where_ref, *refs):
    lhs_refs, part_refs = refs[:grp_count], refs[grp_count:-2]
    out_ref, lhs = refs[-2:]
    group, chip = where_ref[0], where_ref[1]
    rows_each = lhs_refs[0].shape[0]
    per_group = where_ref.shape[0] - 2
    block = rows_each // per_group
    places = []
    for j in range(grp_count):
        lhs[j * rows_each:(j + 1) * rows_each, :] = lhs_refs[j][...]
        for q in range(per_group):
            at = jnp.bitwise_xor(jnp.bitwise_xor(group, j) * per_group + q, chip)
            places.append(pl.ds(pl.multiple_of(at * block, 8), block))
    padded = out_ref.shape[1]
    size = part_refs[0].shape[0] * part_refs[0].shape[1]
    for first in range(0, padded, TILE_N):
        last = min(first + TILE_N, padded)
        total = None
        for i, part_ref in enumerate(part_refs):
            right = part_ref[:, :, first:last].reshape(size, last - first)
            term = jnp.dot(lhs[:, i * size:(i + 1) * size], right, preferred_element_type=jnp.float32)
            total = term if total is None else total + term
        for i, rows in enumerate(places):
            out_ref[rows, first:last] = total[i * block:(i + 1) * block]


def encode(part, lane, at, exponents):
    top = jnp.maximum(jnp.max(jnp.abs(part), axis=1, keepdims=True), 1e-30)
    level = jnp.ceil(jnp.log2(top) * STEPS + 0.05)
    code = jnp.round(part * (jnp.exp2(level * (-1.0 / STEPS)) * QMAX))
    return code, jnp.where(lane == at, level, exponents)


def scale_of(ref):
    last = ref[:, ref.shape[1] - LANES:].astype(jnp.float32)
    return jnp.exp2(last * (1.0 / STEPS)) * (1.0 / QMAX)


def code_kernel(width, split, mine_ref, theirs_ref, own_ref, next_ref, *refs):
    count, padded = mine_ref.shape
    block = own_ref.shape[0]
    chips = count // block
    low_refs, high_refs = refs[:chips - 2], refs[chips - 2:]
    lane = lax.broadcasted_iota(jnp.int32, (count, LANES), 1)
    spare = width % LANES
    exponents = jnp.zeros((count, LANES), jnp.float32)
    for n in range(0, padded, LANES):
        part = mine_ref[:, n:n + LANES] + theirs_ref[:, n:n + LANES]
        own_ref[:, n:n + LANES] = part[:block]
        code, exponents = encode(part, lane, spare + n // LANES, exponents)
        if n + LANES == padded:
            code = jnp.where(lane >= spare, exponents, code)
        code = code.astype(jnp.int16)
        next_ref[:, n:n + LANES] = code[block:2 * block]
        for r in range(2, chips):
            rows = slice(r * block, (r + 1) * block)
            if n < split:
                low_refs[r - 2][:, n:n + LANES] = code[rows]
            elif r % 2 == 0:
                high_refs[r - 2][:, n - split:n - split + LANES] = part[rows]
            else:
                high_refs[r - 2][:, n - split:n - split + LANES] = code[rows]
    exponents = exponents.astype(jnp.int16)
    for r in range(2, chips):
        low_refs[r - 2][:, split:split + LANES] = exponents[r * block:(r + 1) * block]


def relay_kernel(width, split, *refs):
    count = len(refs) // 3
    spare = width % LANES
    for mine_ref, code_ref, out_ref in zip(refs[:count], refs[count:2 * count], refs[2 * count:]):
        block, size = mine_ref.shape
        lane = lax.broadcasted_iota(jnp.int32, (block, LANES), 1)
        scale = scale_of(code_ref)
        exponents = jnp.zeros((block, LANES), jnp.float32)
        for n in range(0, size, LANES):
            at = spare + (n + split) // LANES
            part = mine_ref[:, n:n + LANES] + code_ref[:, n:n + LANES].astype(jnp.float32) * scale[:, at:at + 1]
            if n + LANES == size:
                part = jnp.where(lane < spare, part, 0.0)
            code, exponents = encode(part, lane, at, exponents)
            if n + LANES == size:
                code = jnp.where(lane >= spare, exponents, code)
            out_ref[:, n:n + LANES] = code.astype(jnp.int16)


def combine_kernel(width, split, own_ref, next_ref, *refs):
    out_ref = refs[-1]
    cut = 2 * (len(refs) - 1) // 3
    lows, highs = refs[:cut], refs[cut:-1]
    next_scale = scale_of(next_ref)
    low_scales = [scale_of(ref) for ref in lows]
    high_scales = [scale_of(ref) for ref in highs]
    for low in range(0, width, LANES):
        high = min(low + LANES, width)
        at = width % LANES + low // LANES
        value = own_ref[:, low:high] + next_ref[:, low:high].astype(jnp.float32) * next_scale[:, at:at + 1]
        some, scales, base = (lows, low_scales, 0) if low < split else (highs, high_scales, split)
        for scale, ref in zip(scales, some):
            value = value + ref[:, low - base:high - base].astype(jnp.float32) * scale[:, at:at + 1]
        out_ref[:, low:high] = value


def shards(t_amps, vvvv, irreps):
    mem_count = lax.axis_size("mem")
    grp_count = lax.axis_size("grp")
    per_device, cw, nv = t_amps.shape
    chips = mem_count // 2
    cc = cw // chips
    half = cc // 2
    width = vvvv.shape[1]
    padded = round_up(width, LANES)
    depth = round_up(nv, LANES)
    a_local = width // nv
    mem = lax.axis_index("mem")
    group = lax.axis_index("grp")
    chip, core = mem // 2, mem % 2

    def swap(x, axis, k, count):
        return lax.ppermute(x, axis, [(i, i ^ k) for i in range(count)])

    hop = grp_count // 2

    def mask(source, owner, base, count):
        where = jnp.stack([owner * half + base, group * a_local]).astype(jnp.int32)
        blocks = pltpu.with_memory_space_constraint(source.reshape(half, nv, width), pltpu.HBM)
        return pl.pallas_call(
            lambda *refs: mask_kernel(base, *refs),
            in_specs=[SMEM, SMEM, VMEM, pl.BlockSpec(memory_space=pl.ANY)],
            out_specs=VMEM,
            out_shape=jax.ShapeDtypeStruct((count, depth, padded), jnp.bfloat16),
            scratch_shapes=[
                pltpu.VMEM((depth, LANES), jnp.int32),
                pltpu.VMEM((count, nv, round_up(width // 2, LANES)), jnp.bfloat16),
                pltpu.VMEM((count, nv, width - round_up(width // 2, LANES)), jnp.bfloat16),
                pltpu.SemaphoreType.DMA((2 * count,)),
            ],
            compiler_params=pltpu.CompilerParams(vmem_limit_bytes=16 * 2**20),
            cost_estimate=pl.CostEstimate(flops=0, bytes_accessed=4 * count * nv * width, transcendentals=0),
        )(where, irreps, irreps.reshape(1, nv), blocks)

    split = half // 2
    raw = t_amps.reshape(per_device, chips, 2, half, nv)
    kept = lax.dynamic_index_in_dim(raw, core, 2, keepdims=False)
    lent = swap(lax.dynamic_index_in_dim(raw, 1 - core, 2, keepdims=False), "mem", 1, mem_count)
    even = core == 0
    both = jnp.concatenate([jnp.where(even, kept, lent), jnp.where(even, lent, kept)])
    taken = [lax.dynamic_index_in_dim(both, jnp.bitwise_xor(chip, r), 1, keepdims=False) for r in range(chips)]
    got = [taken[0]] + [swap(taken[r], "mem", 2 * r, mem_count) for r in range(1, chips)]

    def beside(x):
        return [swap(x, "grp", 1, grp_count), swap(x, "grp", 2, grp_count)]

    def corner(near, far):
        cut = near.shape[0] // 2
        return jnp.concatenate([swap(near[:cut], "grp", 2, grp_count), swap(far[cut:], "grp", 1, grp_count)])

    def around(x):
        return [x] + [swap(x, "grp", k, grp_count) for k in range(1, grp_count)]

    def in_order(some):
        bit = 1
        while bit < len(some):
            flip = jnp.bitwise_and(chip, bit) != 0
            some = [jnp.where(flip, some[j ^ bit], some[j]) for j in range(len(some))]
            bit *= 2
        return jnp.concatenate(some)

    x = in_order(got[:chips // 2])
    y = in_order(got[chips // 2:])
    x_all = around(x)
    y, late, x_all[3] = lax.optimization_barrier((y, vvvv, x_all[3]))
    parts = [mask(late, mem, 0, half)]
    x_all, parts = lax.optimization_barrier((x_all, parts))
    y_all, parts = lax.optimization_barrier((around(y), parts))
    halves = [x_all, y_all]

    pair_rows = 2 * per_device
    kept_lhs, lent_lhs = [], []
    is_upper = chip // (chips // 2)
    for one, two in zip(*halves):
        for lhs, target in ((kept_lhs, core), (lent_lhs, 1 - core)):
            if chips // 2 == hop:
                rows = [jnp.where(is_upper == target, one, two)]
            else:
                near, far = [x.reshape(chips // 2, pair_rows, half, nv) for x in (one, two)]
                wanted = target == 0
                rows = []
                for upper in (0, 1):
                    stack = jnp.where(is_upper == upper, near, far)
                    rows += [jnp.where(wanted, stack[j], stack[j + hop]) for j in range(chips // 2) if j // hop % 2 == 0]
            filled = jnp.pad(jnp.concatenate(rows), ((0, 0), (0, 0), (0, depth - nv)))
            lhs.append(filled.reshape(chips // 2 * pair_rows, half * depth))

    rows = grp_count * chips // 2 * pair_rows
    block = hop * pair_rows
    where = jnp.stack([group, chip] + [0] * (chips // grp_count)).astype(jnp.int32)

    def multiply(lhs):
        return pl.pallas_call(
            lambda *refs: dot_kernel(grp_count, *refs),
            in_specs=[SMEM] + [VMEM] * (grp_count + len(parts)),
            out_specs=VMEM,
            out_shape=jax.ShapeDtypeStruct((rows, padded), jnp.float32),
            scratch_shapes=[pltpu.VMEM((rows, half * depth), jnp.bfloat16)],
            compiler_params=pltpu.CompilerParams(vmem_limit_bytes=round_up(rows * half * depth * 6, 2**20) + 6 * 2**20),
            cost_estimate=pl.CostEstimate(flops=2 * rows * half * nv * width, bytes_accessed=4 * rows * width, transcendentals=0),
        )(where, *lhs, *parts)

    theirs = swap(multiply(lent_lhs), "mem", 1, mem_count)
    split = padded // LANES // 2 * LANES
    far_rounds = range(2, chips)
    outs = pl.pallas_call(
        lambda *refs: code_kernel(width, split, *refs),
        in_specs=[VMEM] * 2,
        out_specs=[VMEM] * (2 + 2 * len(far_rounds)),
        out_shape=[
            jax.ShapeDtypeStruct((block, padded), jnp.float32),
            jax.ShapeDtypeStruct((block, padded), jnp.int16),
        ]
        + [jax.ShapeDtypeStruct((block, split + LANES), jnp.int16) for r in far_rounds]
        + [jax.ShapeDtypeStruct((block, padded - split), jnp.int16 if r % 2 else jnp.float32) for r in far_rounds],
        compiler_params=pltpu.CompilerParams(vmem_limit_bytes=16 * 2**20),
    )(multiply(kept_lhs), theirs)
    own, beside_code = outs[:2]
    lows = dict(zip(far_rounds, outs[2:]))
    highs = dict(zip(far_rounds, outs[2 + len(far_rounds):]))
    evens = [r for r in far_rounds if r % 2 == 0]

    helped = [swap(highs[r + 1], "mem", 2, mem_count) for r in evens]
    near_arrived = swap(beside_code, "mem", 2, mem_count)
    arrived = [swap(lows[r], "mem", 2 * r, mem_count) for r in far_rounds]
    relayed = pl.pallas_call(
        lambda *refs: relay_kernel(width, split, *refs),
        in_specs=[VMEM] * (2 * len(evens)),
        out_specs=[VMEM] * len(evens),
        out_shape=[jax.ShapeDtypeStruct((block, padded - split), jnp.int16)] * len(evens),
        compiler_params=pltpu.CompilerParams(vmem_limit_bytes=8 * 2**20),
    )(*[highs[r] for r in evens], *helped)
    high_arrived = [swap(relayed[i], "mem", 2 * r, mem_count) for i, r in enumerate(evens)]
    return pl.pallas_call(
        lambda *refs: combine_kernel(width, split, *refs),
        in_specs=[VMEM] * (2 + len(far_rounds) + len(evens)),
        out_specs=VMEM,
        out_shape=jax.ShapeDtypeStruct((block, width), jnp.float32),
        compiler_params=pltpu.CompilerParams(vmem_limit_bytes=8 * 2**20),
    )(own, near_arrived, *arrived, *high_arrived)


def solution(mesh):
    in_specs = (P(("grp", "mem"), None, None), P("mem", "grp"), P())
    out_specs = P("mem", "grp")
    return jax.shard_map(shards, mesh=mesh, in_specs=in_specs, out_specs=out_specs, check_vma=False)
```
